512 devices in a mesh: tm: 16 (over z, x_lo), lon: 32 (over x_hi, y, core).
Axes of the slice: x: 4 (x_hi: 2, x_lo: 2; x = x_hi * 2 + x_lo), y: 8, z: 8, core: 2. Of those that a mesh axis runs over, the one named last changes fastest.
Arguments:
- latent: bfloat16 [16, 32, 256, 1152], P('tm', None, 'lon'), may hold values from -6 to 6
- timestep: int32 [1], replicated, may hold values from 0 to 29
- modulation: float32 [30, 6, 1152], replicated, may hold values from -3 to 3
- window_offset: int32 [16], P('tm'), may hold values from 0 to 15
- intersection_weight: int32 [32, 32], replicated, may hold values from 1 to 9
- spatial_in: bfloat16 [1152, 1728], P('tm'), may hold values from -0.1875 to 0.1875
- spatial_gain: float32 [2, 72], replicated, may hold values from 1.2 to 2.2
- spatial_out: bfloat16 [576, 1152], P('tm'), may hold values from -0.25 to 0.25
- temporal_in: bfloat16 [1152, 1728], P('tm'), may hold values from -0.1875 to 0.1875
- temporal_gain: float32 [2, 72], replicated, may hold values from 1.2 to 2.2
- temporal_out: bfloat16 [576, 1152], P('tm'), may hold values from -0.25 to 0.25
Outputs:
- updated: bfloat16 [16, 32, 256, 1152], P('tm', None, 'lon')
The draws below stay inside these ranges and needn't reach their ends.
All inputs are finite; a program needn't handle non-finite values.
Results may differ from the reference program's by a relative error of at most 0.02.
Values may be sent and summed in bfloat16 or wider, within the bound.
A program may use at most 128 MiB of HBM per device.

```python
import math
import jax
import jax.numpy as jnp
from jax import lax

D = 1152
HEADS = 8
HEAD_DIM = 72
HD = 576
ROWS = 32
WIN = 32
STRIDE = 16
NSTEPS = 30
COL_DEV = 8
FRAMES = 16
COLS = 256
N_LON = 32


def touch_ends(entries, own_key, smallest, top_value):
    longest = entries.shape.index(max(entries.shape))
    spots = []
    for shift in (0, 1):
        where = [jax.random.randint(jax.random.fold_in(own_key, axis), (), 0, length) for axis, length in enumerate(entries.shape)]
        where[longest] = (where[longest] + shift) % entries.shape[longest]
        spots.append(tuple(where))
    return entries.at[spots[0]].set(smallest).at[spots[1]].set(top_value)


def shard_levels(key, extent, split, smallest, top_value):
    level = 1.0
    for dim, blocks in split:
        heights = jax.random.uniform(jax.random.fold_in(jax.random.fold_in(key, 6), dim), (blocks,), jnp.float32, smallest / len(split), top_value / len(split))
        level = level * jnp.repeat(jnp.exp(heights), extent[dim] // blocks).reshape((-1,) + (1,) * (len(extent) - 1 - dim))
    return level


def noise(rng, shape, scale, most, pieces=(), kind=jnp.bfloat16):
    drawn = jax.random.normal(rng, shape, jnp.float32) * scale
    if len(pieces) > 0:
        drawn = shard_levels(rng, shape, pieces, -0.22, 0.18) * drawn
    return jnp.clip(drawn, min=-most, max=most).astype(kind)


def setup_inputs(seed: int = 0) -> dict:
    splits = jax.random.split(jax.random.key(seed), 12)
    latent = noise(splits[0], (FRAMES, ROWS, COLS, D), 1.0, 6.0, ((0, 16), (2, 32)))
    timestep = jax.random.randint(splits[1], (1,), 0, NSTEPS).astype(jnp.int32)
    modulation = noise(splits[2], (NSTEPS, 6, D), 0.5, 3.0, (), jnp.float32)
    window_offset = touch_ends(jax.random.randint(splits[3], (FRAMES,), 0, STRIDE), jax.random.fold_in(splits[3], 1), 0, STRIDE - 1).astype(jnp.int32)
    intersection_weight = touch_ends(jax.random.randint(splits[4], (ROWS, WIN), 1, 10), jax.random.fold_in(splits[4], 1), 1, 9).astype(jnp.int32)
    spatial_in = noise(splits[5], (D, 3 * HD), D ** -0.5, 0.1875, ((0, 16),))
    spatial_gain = jnp.clip(jnp.exp(jax.random.uniform(splits[6], (2, HEAD_DIM), jnp.float32, math.log(1.2), math.log(2.2))), 1.2, 2.2)
    spatial_out = noise(splits[7], (HD, D), HD ** -0.5, 0.25, ((0, 16),))
    temporal_in = noise(splits[8], (D, 3 * HD), D ** -0.5, 0.1875, ((0, 16),))
    temporal_gain = jnp.clip(jnp.exp(jax.random.uniform(splits[9], (2, HEAD_DIM), jnp.float32, math.log(1.2), math.log(2.2))), 1.2, 2.2)
    temporal_out = noise(splits[10], (HD, D), HD ** -0.5, 0.25, ((0, 16),))
    return dict(latent=latent, timestep=timestep, modulation=modulation, window_offset=window_offset, intersection_weight=intersection_weight, spatial_in=spatial_in, spatial_gain=spatial_gain, spatial_out=spatial_out, temporal_in=temporal_in, temporal_gain=temporal_gain, temporal_out=temporal_out)


def layer_norm(values):
    values = values.astype(jnp.float32)
    center = values - lax.optimization_barrier(jnp.mean(values, axis=-1, keepdims=True))
    spread = lax.optimization_barrier(jnp.mean(center * center, axis=-1, keepdims=True))
    return center / jnp.sqrt(spread + 1e-06)

def head_norm(projected_block, gain_row, factor):
    shaped = projected_block.reshape(projected_block.shape[:-1] + (HEADS, HEAD_DIM))
    mean_square = lax.optimization_barrier(jnp.mean(shaped * shaped, axis=-1, keepdims=True))
    normed = shaped / jnp.sqrt(mean_square + 1e-06) * gain_row * factor
    return normed.reshape(projected_block.shape).astype(jnp.bfloat16)

def split_heads(projected, gain_table):
    queries = head_norm(projected[..., :HD], gain_table[0], HEAD_DIM ** (-0.5))
    key_rows = head_norm(projected[..., HD:2 * HD], gain_table[1], 1.0)
    values = projected[..., 2 * HD:].astype(jnp.bfloat16)
    return (queries, key_rows, values)

def reference(latent, timestep, modulation, window_offset, intersection_weight, spatial_in, spatial_gain, spatial_out, temporal_in, temporal_gain, temporal_out):
    modulators = modulation[timestep[0]]
    flattened = latent.reshape(-1, D)
    normed_in = (layer_norm(flattened) * (1.0 + modulators[1]) + modulators[0]).astype(jnp.bfloat16)
    projected = jnp.dot(normed_in, spatial_in, preferred_element_type=jnp.float32)
    queries, key_rows, values = split_heads(projected, spatial_gain)
    grid_shape = (FRAMES, ROWS, COLS, HD)
    queries = queries.reshape(grid_shape)
    key_rows = key_rows.reshape(grid_shape)
    values = values.reshape(grid_shape)
    reach = (WIN + COL_DEV - 2) // COL_DEV
    relative = jnp.arange(-reach * COL_DEV, (reach + 1) * COL_DEV).astype(jnp.int32)
    inside = jnp.arange(COL_DEV).astype(jnp.int32)
    positions = jnp.arange(WIN).astype(jnp.int32)
    weight_table = intersection_weight.astype(jnp.float32)
    span = relative.shape[0]

    def window_block(index):
        frame = index // N_LON
        strip = index % N_LON
        column = strip * COL_DEV + inside
        phase_pos = jnp.mod(column - window_offset[frame], STRIDE)
        second_start = inside - phase_pos
        first_start = second_start - STRIDE
        first_mask = ((relative[None, :] >= first_start[:, None]) & (relative[None, :] < first_start[:, None] + WIN)).astype(jnp.float32)
        second_mask = ((relative[None, :] >= second_start[:, None]) & (relative[None, :] < second_start[:, None] + WIN)).astype(jnp.float32)
        second_weight = lax.optimization_barrier(jnp.sum(jnp.where(positions[None, None, :] == phase_pos[None, :, None], weight_table[:, None, :], 0.0), axis=-1))
        first_weight = lax.optimization_barrier(jnp.sum(jnp.where(positions[None, None, :] == phase_pos[None, :, None] + STRIDE, weight_table[:, None, :], 0.0), axis=-1))
        first_share = first_weight / (first_weight + second_weight)
        second_share = second_weight / (first_weight + second_weight)
        source = jnp.mod(strip * COL_DEV + relative, COLS).astype(jnp.int32)
        frame_queries = lax.dynamic_index_in_dim(queries, frame, 0, keepdims=False)
        frame_queries = lax.dynamic_slice_in_dim(frame_queries, strip * COL_DEV, COL_DEV, 1)
        frame_keys = jnp.take(lax.dynamic_index_in_dim(key_rows, frame, 0, keepdims=False), source, axis=1)
        frame_values = jnp.take(lax.dynamic_index_in_dim(values, frame, 0, keepdims=False), source, axis=1)
        query_heads = frame_queries.reshape(ROWS, COL_DEV, HEADS, HEAD_DIM).astype(jnp.float32)
        key_heads = frame_keys.reshape(ROWS, span, HEADS, HEAD_DIM).astype(jnp.float32)
        value_heads = frame_values.reshape(ROWS, span, HEADS, HEAD_DIM).astype(jnp.float32)
        scores = jnp.einsum('rjhd,suhd->hrjsu', query_heads, key_heads)
        powers = jnp.exp(scores)
        first_full = first_mask[None, None, :, None, :]
        second_full = second_mask[None, None, :, None, :]
        first_total = lax.optimization_barrier(jnp.sum(powers * first_full, axis=(3, 4)))
        second_total = lax.optimization_barrier(jnp.sum(powers * second_full, axis=(3, 4)))
        blend = (first_share[None] / first_total)[..., None, None] * first_full + (second_share[None] / second_total)[..., None, None] * second_full
        mixture = (powers * blend).astype(jnp.bfloat16)
        attended = jnp.einsum('hrjsu,suhd->rjhd', mixture.astype(jnp.float32), value_heads)
        return attended.astype(jnp.bfloat16).reshape(ROWS, COL_DEV, HD)
    blocks = lax.map(window_block, jnp.arange(FRAMES * N_LON).astype(jnp.int32))
    blocks = blocks.reshape(FRAMES, N_LON, ROWS, COL_DEV, HD)
    spatial_result = jnp.transpose(blocks, (0, 2, 1, 3, 4)).reshape(-1, HD)
    middle = (flattened.astype(jnp.float32) + modulators[2] * jnp.dot(spatial_result, spatial_out, preferred_element_type=jnp.float32)).astype(jnp.bfloat16)
    normed_mid = (layer_norm(middle) * (1.0 + modulators[4]) + modulators[3]).astype(jnp.bfloat16)
    projected_time = jnp.dot(normed_mid, temporal_in, preferred_element_type=jnp.float32)
    time_query, time_key, time_value = split_heads(projected_time, temporal_gain)
    time_shape = (FRAMES, ROWS * COLS, HEADS, HEAD_DIM)
    scores_time = jnp.einsum('fphd,gphd->phfg', time_query.reshape(time_shape).astype(jnp.float32), time_key.reshape(time_shape).astype(jnp.float32))
    powers_time = jnp.exp(scores_time)
    mixture_time = (powers_time / lax.optimization_barrier(jnp.sum(powers_time, axis=-1, keepdims=True))).astype(jnp.bfloat16)
    attended_time = jnp.einsum('phfg,gphd->fphd', mixture_time.astype(jnp.float32), time_value.reshape(time_shape).astype(jnp.float32))
    temporal_result = attended_time.astype(jnp.bfloat16).reshape(-1, HD)
    updated = (middle.astype(jnp.float32) + modulators[5] * jnp.dot(temporal_result, temporal_out, preferred_element_type=jnp.float32)).astype(jnp.bfloat16)
    return updated.reshape(latent.shape)
```

```python
import functools
import math

import jax
import jax.numpy as jnp
from jax import lax
from jax.experimental import pallas as pl
from jax.experimental.pallas import tpu as pltpu
from jax.sharding import PartitionSpec as P

D = 1152
HEADS = 8
HEAD_DIM = 72
HD = 576
HP = 640
ROWS = 32
COLS = 8
TOK = ROWS * COLS
WIN = 32
STRIDE = 16
BF = jnp.bfloat16
F32 = jnp.float32
MESH = pl.DeviceIdType.MESH
LOG2E = math.log2(math.e)


def iota(shape, dim):
    return lax.broadcasted_iota(jnp.int32, shape, dim)


def dot(a, b):
    return jnp.dot(a, b, preferred_element_type=F32)


def dot_t(a, b):
    return lax.dot_general(a, b, (((1,), (1,)), ((), ())), preferred_element_type=F32)


def layer_norm(x):
    center = x - jnp.mean(x, axis=-1, keepdims=True)
    spread = jnp.mean(center * center, axis=-1, keepdims=True)
    return center * lax.rsqrt(spread + 1e-06)


def head_norm(p, gain, seg, seg_t):
    square = dot((p * p).astype(BF), seg) * (1.0 / HEAD_DIM) + 1e-06
    inverse = lax.rsqrt(square)
    high = inverse.astype(BF)
    low = (inverse - high.astype(F32)).astype(BF)
    spread = dot(jnp.concatenate([high, low], axis=1), seg_t)
    return (p * spread * gain).astype(BF)


def kernel(
    lat_ref, ts_ref, mod_ref, off_ref, iw_ref, si_ref, sg_ref, so_ref, ti_ref, tg_ref, to_ref,
    out_ref,
    w_si, w_so, w_ti, w_to, w_spat, w_temp, wo_spat, wo_temp,
    seg, seg_t, gains, gpad, latp, xs, qbuf, kbuf, vbuf, kcell, vcell, att, mid, nm, xt, tqkv, tsend, rt,
    w_send, w_recv, s_send, s_recv, kv_send, kv_recv, a_send, a_recv, r_send, r_recv, loc,
):
    t = lax.axis_index("tm")
    l = lax.axis_index("lon")
    nlon = lax.axis_size("lon")
    ntm = lax.axis_size("tm")
    nz, nq = ntm // 2, nlon // 2
    ny = nq // 2
    z, xl = t // 2, lax.rem(t, 2)
    q, c = l // 2, lax.rem(l, 2)
    xh, y = q // ny, lax.rem(q, ny)
    d = 1 - 2 * c

    def dev(tm, lon):
        return {"tm": tm, "lon": lon}

    def around(step):
        x = lax.rem(xh * 2 + xl + step + 4, 4)
        return dev(z * 2 + lax.rem(x, 2), ((x // 2) * ny + y) * 2 + c)

    zn = dev(lax.rem(z + d + nz, nz) * 2 + xl, l)
    xn = around(d)
    xp = around(-d)
    sib = dev(t, q * 2 + 1 - c)
    east = dev(t, lax.rem(q + 1, nq) * 2 + c)
    west = dev(t, lax.rem(q + nq - 1, nq) * 2 + c)

    barrier = pltpu.get_barrier_semaphore()
    others = [dev(lax.rem(t + k, ntm), l) for k in range(1, 16)] + [sib, east, west]
    across_x = lax.rem(xh * 2 + xl + jnp.where(xl == 0, 3, 1), 4)
    across = dev(z * 2 + lax.rem(across_x, 2), ((across_x // 2) * ny + y) * 2 + c)
    others.append(across)
    for other in others:
        pl.semaphore_signal(barrier, inc=1, device_id=other, device_id_type=MESH)

    weights = (w_si, w_so, w_ti, w_to)
    sources = (si_ref, so_ref, ti_ref, to_ref)
    own = [pltpu.make_async_copy(sources[a], weights[a].at[t], loc.at[a]) for a in range(4)]
    for copy in own:
        copy.start()

    pl.semaphore_wait(barrier, len(others))

    sent = []

    def wcopy(a, slot, sem, target):
        return pltpu.make_async_remote_copy(
            src_ref=weights[a].at[slot], dst_ref=weights[a].at[slot],
            send_sem=w_send.at[a, sem], recv_sem=w_recv.at[a, slot],
            device_id=target, device_id_type=MESH,
        )

    def mine(i, plane):
        return lax.rem(z - d * (i + c) + 2 * nz, nz) * 2 + plane

    def theirs(i, plane):
        return lax.rem(z + d * (i + 1 - c) + 2 * nz, nz) * 2 + plane

    def send(a, slot, sem, target):
        copy = wcopy(a, slot, sem, target)
        copy.start()
        sent.append(copy)

    def gather_start(a):
        own[a].wait()

        @pl.when(c == 1)
        def _():
            wcopy(a, t, 3, zn).start()

    def gather_a(a, i):
        slot = mine(i, xl)
        if i == 0:

            @pl.when(c == 1)
            def _():
                wcopy(a, slot, 0, zn).wait_recv()
                wcopy(a, slot, 8, sib).start()

        else:
            wcopy(a, slot, 0, zn).wait_recv()
            send(a, slot, 8 + i, sib)
        if i < 3:
            send(a, slot, i, zn)
        send(a, slot, 4 + i, xn)

    def gather_b(a, i):
        slot = mine(i, 1 - xl)
        wcopy(a, slot, 0, zn).wait_recv()
        send(a, slot, 12 + i, sib)

    def gather_rest(a):
        for i in range(4):
            slot = theirs(i, xl)
            if i == 0:

                @pl.when(c == 0)
                def _():
                    wcopy(a, slot, 0, zn).wait_recv()

            else:
                wcopy(a, slot, 0, zn).wait_recv()
            wcopy(a, theirs(i, 1 - xl), 0, zn).wait_recv()

    def gather_end(a):
        @pl.when(c == 1)
        def _():
            wcopy(a, t, 3, zn).wait_send()
            wcopy(a, mine(0, xl), 8, sib).wait_send()

    def arrange_in(source, target):
        @pl.loop(0, 8)
        def _(pair):
            rows = pl.ds(pl.multiple_of(pair * 144, 16), 144)
            both = jnp.concatenate(
                [source[2 * pair].astype(F32), source[2 * pair + 1].astype(F32)], axis=0
            )
            for part in range(3):
                cut = both[:, part * HD : (part + 1) * HD]
                wide = jnp.concatenate([cut, jnp.zeros((144, HP - HD), F32)], axis=1)
                target[part, rows, :] = wide.astype(BF)

    def arrange_out(source, target):
        for four in range(4):
            block = jnp.concatenate([source[4 * four + k].astype(F32) for k in range(4)], axis=0)
            target[144 * four : 144 * (four + 1), :] = block.astype(BF)
        target[HD:HP, :] = jnp.zeros((HP - HD, D), BF)

    gather_start(0)
    gather_a(0, 0)

    steps = mod_ref.shape[0]
    chosen = (iota((steps, 6, D), 0) == ts_ref[0]).astype(F32)
    modulators = jnp.sum(mod_ref[...] * chosen, axis=0)
    there = iota((TOK, TOK), 1)
    here = iota((TOK, TOK), 0)
    perm = (there == (here & 31) * COLS + (here >> 5)).astype(F32).astype(BF)
    ordered = dot(perm, lat_ref[...])
    latp[...] = ordered.astype(BF)
    xs[2] = (layer_norm(ordered) * (1.0 + modulators[1:2]) + modulators[0:1]).astype(BF)

    HALF = TOK // 2

    def scopy(source, hop, side, half):
        part = pl.ds(half * HALF, HALF)
        slot = 2 - hop if side == 0 else 2 + hop
        return pltpu.make_async_remote_copy(
            src_ref=xs.at[source, part], dst_ref=xs.at[slot, part],
            send_sem=s_send.at[2 * (hop - 1) + side, half],
            recv_sem=s_recv.at[2 * (hop - 1) + side, half],
            device_id=east if side == 0 else west, device_id_type=MESH,
        )

    def strip_send(hop, half):
        for side in (0, 1):
            source = 2 if hop == 1 else (1 if side == 0 else 3)
            if hop == 2:
                scopy(2, 1, side, half).wait_recv()
            copy = scopy(source, hop, side, half)
            copy.start()
            sent.append(copy)

    strip_send(1, 0)
    strip_send(1, 1)

    kbuf[9 * COLS :] = jnp.zeros((COLS, ROWS, HP), BF)
    vbuf[9 * COLS :] = jnp.zeros((COLS, ROWS, HP), BF)

    lane = iota((HP, 128), 0)
    head = iota((HP, 128), 1) * HEAD_DIM
    seg[...] = ((lane >= head) & (lane < head + HEAD_DIM)).astype(F32).astype(BF)
    lane = iota((256, HP), 1)
    head = (iota((256, HP), 0) & 127) * HEAD_DIM
    seg_t[...] = ((lane >= head) & (lane < head + HEAD_DIM)).astype(F32).astype(BF)
    gpad[...] = jnp.zeros_like(gpad)
    gpad[0:2, 0:HEAD_DIM] = sg_ref[...]
    gpad[2:4, 0:HEAD_DIM] = tg_ref[...]
    lane = iota((128, HP), 1)
    within = lane
    for h in range(1, HEADS):
        within = jnp.where(lane >= h * HEAD_DIM, lane - h * HEAD_DIM, within)
    spread = (within == iota((128, HP), 0)).astype(F32)
    gains[...] = jnp.dot(
        gpad[...], spread, preferred_element_type=F32, precision=lax.Precision.HIGHEST
    )
    factor = HEAD_DIM ** (-0.5) * LOG2E

    gather_a(0, 1)
    gather_b(0, 0)
    gather_a(0, 2)
    gather_b(0, 1)
    strip_send(2, 0)
    gather_a(0, 3)
    gather_b(0, 2)
    gather_start(1)
    gather_a(1, 0)
    strip_send(2, 1)
    gather_b(0, 3)
    gather_a(1, 1)
    gather_b(1, 0)
    gather_a(1, 2)
    gather_b(1, 1)
    gather_rest(0)
    gather_start(2)
    gather_start(3)
    gather_a(2, 0)
    gather_a(3, 0)
    arrange_in(w_si, w_spat)

    qbuf[...] = head_norm(dot(xs[2], w_spat[0]), gains[0:1] * factor, seg[...], seg_t[...])
    gather_a(1, 3)
    gather_b(1, 2)

    def keys_values(slot):
        cols = pl.ds(slot * (2 * COLS), COLS)
        x = xs[slot]
        keys = head_norm(dot(x, w_spat[1]), gains[1:2], seg[...], seg_t[...])
        kbuf[cols] = keys.reshape(COLS, ROWS, HP)
        vbuf[cols] = dot(x, w_spat[2]).astype(BF).reshape(COLS, ROWS, HP)

    def kv_copies(order):
        target = 2 * order + 1
        source = target + 1 - 2 * c
        src = pl.ds(source * COLS, COLS)
        dst = pl.ds(target * COLS, COLS)
        return [
            pltpu.make_async_remote_copy(
                src_ref=buf.at[src], dst_ref=buf.at[dst], send_sem=kv_send.at[j, order],
                recv_sem=kv_recv.at[j, order], device_id=sib, device_id_type=MESH,
            )
            for j, buf in enumerate((kbuf, vbuf))
        ]

    def kv_share(order):
        for copy in kv_copies(order):
            copy.start()
            sent.append(copy)

    @pl.loop(0, 3)
    def _(i):
        keys_values(2 - lax.rem(i, 2) + i // 2)

    kv_share(1)
    kv_share(2)
    kv_share(3 * c)
    gather_b(1, 3)
    gather_rest(1)
    arrange_out(w_so, wo_spat)
    gather_a(2, 1)
    gather_a(3, 1)
    gather_b(2, 0)
    gather_b(3, 0)
    for half in (0, 1):
        for side in (0, 1):
            scopy(2, 2, side, half).wait_recv()

    @pl.loop(0, 2)
    def _(i):
        keys_values(4 * i)

    kv_share(3 - 3 * c)
    gather_a(2, 2)
    gather_a(3, 2)
    gather_b(2, 1)
    gather_b(3, 1)

    shift = lax.rem(COLS * l - off_ref[0] + STRIDE, STRIDE)
    table = iw_ref[...].astype(F32)
    place = iota((ROWS, WIN), 1)
    second, first = [], []
    for col in range(COLS):
        m = lax.rem(shift + col, STRIDE)
        second.append(jnp.sum(jnp.where(place == m, table, 0.0), axis=1, keepdims=True))
        first.append(jnp.sum(jnp.where(place == m + STRIDE, table, 0.0), axis=1, keepdims=True))
    second = jnp.concatenate(second, axis=0)
    first = jnp.concatenate(first, axis=0)
    share_first = first / (first + second)
    share_second = second / (first + second)
    early = (shift + (iota((TOK, 1), 0) >> 5)) < STRIDE

    for order in range(4):
        for copy in kv_copies(order):
            copy.wait_recv()

    CELL = STRIDE * ROWS
    for col in range(4 * STRIDE):
        rows = slice(col * ROWS, (col + 1) * ROWS)
        kcell[rows, :] = kbuf[col + STRIDE - shift]
        vcell[rows, :] = vbuf[col + STRIDE - shift]

    def window(h):
        w = pl.multiple_of(((9 * h) // 16) * 128, 128)
        off = HEAD_DIM * h - w
        lanes = iota((1, 256), 1)
        inside = ((lanes >= off) & (lanes < off + HEAD_DIM)).astype(F32)
        return w, inside

    def spatial_head(h, _):
        w, inside = window(h)
        cols = pl.ds(w, 256)
        inside_b = inside.astype(BF)
        outside_b = (1.0 - inside).astype(BF)
        qh = qbuf[:, cols] * inside_b
        totals, sums = [], []
        for g in range(4):
            rows = slice(g * CELL, (g + 1) * CELL)
            powers = jnp.exp2(dot_t(qh, kcell[rows, cols])).astype(BF)
            o = dot(powers, vcell[rows, cols] * inside_b + outside_b)
            totals.append(o)
            sums.append(o[:, 255:256])
        near = sums[1] + sums[2]
        ca = share_first / jnp.where(early, sums[0] + sums[1], near)
        cb = share_second / jnp.where(early, near, sums[2] + sums[3])
        cab = ca + cb
        res = (
            jnp.where(early, ca, 0.0) * totals[0]
            + jnp.where(early, cab, ca) * totals[1]
            + jnp.where(early, cb, cab) * totals[2]
            + jnp.where(early, 0.0, cb) * totals[3]
        )
        att[:, cols] = att[:, cols] * (1.0 - inside) + res * inside
        return 0

    att[...] = jnp.zeros_like(att)
    lax.fori_loop(0, 4, spatial_head, 0)
    gather_a(2, 3)
    gather_a(3, 3)
    gather_b(2, 2)
    gather_b(3, 2)
    lax.fori_loop(4, 8, spatial_head, 0)
    gather_b(2, 3)
    gather_b(3, 3)

    middle = latp[...].astype(F32) + modulators[2:3] * dot(att[...].astype(BF), wo_spat[...])
    middle = middle.astype(BF)
    mid[...] = middle
    normed = layer_norm(middle.astype(F32)) * (1.0 + modulators[4:5]) + modulators[3:4]
    nm[...] = normed.astype(BF)

    BAND = TOK // 16
    ORDER = (8, 9, 7, 10, 6, 11, 5, 12, 4, 13, 3, 14, 2, 15, 1)

    def band(index):
        return pl.ds(pl.multiple_of(index * BAND, BAND), BAND)

    def exchange(source, target, send_sems, recv_sems):
        for k in ORDER:
            peer = lax.rem(t + k, ntm)
            copy = pltpu.make_async_remote_copy(
                src_ref=source.at[band(peer)], dst_ref=target.at[band(t)],
                send_sem=send_sems.at[k], recv_sem=recv_sems.at[t],
                device_id=dev(peer, l), device_id_type=MESH,
            )
            copy.start()
            sent.append(copy)
        target[band(t), :] = source[band(t), :]

    def exchange_wait(source, target, send_sems, recv_sems):
        for k in range(1, 16):
            peer = lax.rem(t + k, ntm)
            pltpu.make_async_remote_copy(
                src_ref=source.at[band(peer)], dst_ref=target.at[band(peer)],
                send_sem=send_sems.at[k], recv_sem=recv_sems.at[peer],
                device_id=dev(peer, l), device_id_type=MESH,
            ).wait_recv()

    exchange(nm, xt, a_send, a_recv)
    gather_rest(2)
    gather_rest(3)
    arrange_in(w_ti, w_temp)
    arrange_out(w_to, wo_temp)
    exchange_wait(nm, xt, a_send, a_recv)

    x = xt[...]
    tqkv[0] = head_norm(dot(x, w_temp[0]), gains[2:3] * factor, seg[...], seg_t[...])
    tqkv[1] = head_norm(dot(x, w_temp[1]), gains[3:4], seg[...], seg_t[...])
    tqkv[2] = dot(x, w_temp[2]).astype(BF)
    same = ((iota((TOK, TOK), 0) & 15) == (iota((TOK, TOK), 1) & 15)).astype(F32)

    def temporal_head(h, _):
        w, inside = window(h)
        cols = pl.ds(w, 256)
        inside_b = inside.astype(BF)
        outside_b = (1.0 - inside).astype(BF)
        scores = dot_t(tqkv[0, :, cols] * inside_b, tqkv[1, :, cols])
        powers = (jnp.exp2(scores) * same).astype(BF)
        o = dot(powers, tqkv[2, :, cols] * inside_b + outside_b)
        att[:, cols] = att[:, cols] * (1.0 - inside) + o * (inside / o[:, 255:256])
        return 0

    att[...] = jnp.zeros_like(att)
    lax.fori_loop(0, 8, temporal_head, 0)
    tsend[...] = att[...].astype(BF)
    exchange(tsend, rt, r_send, r_recv)
    there = iota((TOK, TOK), 1)
    here = iota((TOK, TOK), 0)
    back = (there == (here & 7) * ROWS + (here >> 3)).astype(F32).astype(BF)
    exchange_wait(tsend, rt, r_send, r_recv)

    result = mid[...].astype(F32) + modulators[5:6] * dot(rt[...], wo_temp[...])
    out_ref[...] = dot(back, result.astype(BF)).astype(BF)

    for copy in sent:
        copy.wait_send()
    for a in range(4):
        gather_end(a)


def local(
    latent,
    timestep,
    modulation,
    window_offset,
    intersection_weight,
    spatial_in,
    spatial_gain,
    spatial_out,
    temporal_in,
    temporal_gain,
    temporal_out,
):
    vmem = pl.BlockSpec(memory_space=pltpu.VMEM)
    smem = pl.BlockSpec(memory_space=pltpu.SMEM)
    hbm = pl.BlockSpec(memory_space=pl.ANY)
    dma = pltpu.SemaphoreType.DMA
    out = pl.pallas_call(
        kernel,
        out_shape=jax.ShapeDtypeStruct((TOK, D), BF),
        in_specs=[vmem, smem, vmem, smem, vmem, hbm, vmem, hbm, hbm, vmem, hbm],
        out_specs=vmem,
        scratch_shapes=[
            pltpu.VMEM((16, 72, 3 * HD), BF),
            pltpu.VMEM((16, 36, D), BF),
            pltpu.VMEM((16, 72, 3 * HD), BF),
            pltpu.VMEM((16, 36, D), BF),
            pltpu.VMEM((3, D, HP), BF),
            pltpu.VMEM((3, D, HP), BF),
            pltpu.VMEM((HP, D), BF),
            pltpu.VMEM((HP, D), BF),
            pltpu.VMEM((HP, 128), BF),
            pltpu.VMEM((256, HP), BF),
            pltpu.VMEM((8, HP), F32),
            pltpu.VMEM((8, 128), F32),
            pltpu.VMEM((TOK, D), BF),
            pltpu.VMEM((5, TOK, D), BF),
            pltpu.VMEM((TOK, HP), BF),
            pltpu.VMEM((10 * COLS, ROWS, HP), BF),
            pltpu.VMEM((10 * COLS, ROWS, HP), BF),
            pltpu.VMEM((8 * TOK, HP), BF),
            pltpu.VMEM((8 * TOK, HP), BF),
            pltpu.VMEM((TOK, HP), F32),
            pltpu.VMEM((TOK, D), BF),
            pltpu.VMEM((TOK, D), BF),
            pltpu.VMEM((TOK, D), BF),
            pltpu.VMEM((3, TOK, HP), BF),
            pltpu.VMEM((TOK, HP), BF),
            pltpu.VMEM((TOK, HP), BF),
            dma((4, 16)),
            dma((4, 16)),
            dma((4, 2)),
            dma((4, 2)),
            dma((2, 4)),
            dma((2, 4)),
            dma((16,)),
            dma((16,)),
            dma((16,)),
            dma((16,)),
            dma((4,)),
        ],
        compiler_params=pltpu.CompilerParams(
            collective_id=0, has_side_effects=True, vmem_limit_bytes=56 << 20
        ),
        cost_estimate=pl.CostEstimate(
            flops=10 * 10**9, bytes_accessed=4 * 10**6, transcendentals=5 * 10**6
        ),
    )(
        latent.reshape(TOK, D),
        timestep,
        modulation,
        window_offset,
        intersection_weight,
        spatial_in,
        spatial_gain,
        spatial_out,
        temporal_in,
        temporal_gain,
        temporal_out,
    )
    return out.reshape(latent.shape)


def solution(mesh):
    in_specs = (
        P("tm", None, "lon", None),
        P(),
        P(),
        P("tm"),
        P(),
        P("tm", None),
        P(),
        P("tm", None),
        P("tm", None),
        P(),
        P("tm", None),
    )
    out_specs = P("tm", None, "lon", None)
    return jax.shard_map(local, mesh=mesh, in_specs=in_specs, out_specs=out_specs, check_vma=False)
```

```python
import functools
import math

import jax
import jax.numpy as jnp
from jax import lax
from jax.experimental import pallas as pl
from jax.experimental.pallas import tpu as pltpu
from jax.sharding import PartitionSpec as P

D = 1152
HEADS = 8
HEAD_DIM = 72
HD = 576
HP = 640
ROWS = 32
COLS = 8
TOK = ROWS * COLS
WIN = 32
STRIDE = 16
BF = jnp.bfloat16
F32 = jnp.float32
MESH = pl.DeviceIdType.MESH
LOG2E = math.log2(math.e)


def iota(shape, dim):
    return lax.broadcasted_iota(jnp.int32, shape, dim)


def dot(a, b):
    return jnp.dot(a, b, preferred_element_type=F32)


def dot_t(a, b):
    return lax.dot_general(a, b, (((1,), (1,)), ((), ())), preferred_element_type=F32)


def layer_norm(x):
    center = x - jnp.mean(x, axis=-1, keepdims=True)
    spread = jnp.mean(center * center, axis=-1, keepdims=True)
    return center * lax.rsqrt(spread + 1e-06)


def head_norm(p, gain, seg, seg_t):
    square = dot((p * p).astype(BF), seg) * (1.0 / HEAD_DIM) + 1e-06
    inverse = lax.rsqrt(square)
    high = inverse.astype(BF)
    low = (inverse - high.astype(F32)).astype(BF)
    spread = dot(jnp.concatenate([high, low], axis=1), seg_t)
    return (p * spread * gain).astype(BF)


def kernel(
    lat_ref, ts_ref, mod_ref, off_ref, iw_ref, si_ref, sg_ref, so_ref, ti_ref, tg_ref, to_ref,
    out_ref,
    w_si, w_so, w_ti, w_to, w_spat, w_temp, wo_spat, wo_temp,
    seg, seg_t, gains, gpad, latp, xs, qbuf, kbuf, vbuf, kcell, vcell, att, mid, nm, xt, tqkv, tsend, rt,
    w_send, w_recv, s_send, s_recv, kv_send, kv_recv, a_send, a_recv, r_send, r_recv, loc,
):
    t = lax.axis_index("tm")
    l = lax.axis_index("lon")
    nlon = lax.axis_size("lon")
    ntm = lax.axis_size("tm")
    nz, nq = ntm // 2, nlon // 2
    ny = nq // 2
    z, xl = t // 2, lax.rem(t, 2)
    q, c = l // 2, lax.rem(l, 2)
    xh, y = q // ny, lax.rem(q, ny)
    d = 1 - 2 * c

    def dev(tm, lon):
        return {"tm": tm, "lon": lon}

    def around(step):
        x = lax.rem(xh * 2 + xl + step + 4, 4)
        return dev(z * 2 + lax.rem(x, 2), ((x // 2) * ny + y) * 2 + c)

    zn = dev(lax.rem(z + d + nz, nz) * 2 + xl, l)
    xn = around(d)
    xp = around(-d)
    sib = dev(t, q * 2 + 1 - c)
    east = dev(t, lax.rem(q + 1, nq) * 2 + c)
    west = dev(t, lax.rem(q + nq - 1, nq) * 2 + c)

    barrier = pltpu.get_barrier_semaphore()
    others = [dev(lax.rem(t + k, ntm), l) for k in range(1, 16)] + [sib, east, west]
    across_x = lax.rem(xh * 2 + xl + jnp.where(xl == 0, 3, 1), 4)
    across = dev(z * 2 + lax.rem(across_x, 2), ((across_x // 2) * ny + y) * 2 + c)
    others.append(across)
    for other in others:
        pl.semaphore_signal(barrier, inc=1, device_id=other, device_id_type=MESH)

    weights = (w_si, w_so, w_ti, w_to)
    sources = (si_ref, so_ref, ti_ref, to_ref)
    own = [pltpu.make_async_copy(sources[a], weights[a].at[t], loc.at[a]) for a in range(4)]
    for copy in own:
        copy.start()

    pl.semaphore_wait(barrier, len(others))

    sent = []

    def wcopy(a, slot, sem, target):
        return pltpu.make_async_remote_copy(
            src_ref=weights[a].at[slot], dst_ref=weights[a].at[slot],
            send_sem=w_send.at[a, sem], recv_sem=w_recv.at[a, slot],
            device_id=target, device_id_type=MESH,
        )

    def mine(i, plane):
        return lax.rem(z - d * (i + c) + 2 * nz, nz) * 2 + plane

    def theirs(i, plane):
        return lax.rem(z + d * (i + 1 - c) + 2 * nz, nz) * 2 + plane

    def send(a, slot, sem, target):
        copy = wcopy(a, slot, sem, target)
        copy.start()
        sent.append(copy)

    pair = dev(z * 2 + 1 - xl, l)

    def ring_slot(k, plane, way):
        return lax.rem(z - way * k + 2 * nz, nz) * 2 + plane

    def ring_start(a):
        own[a].wait()
        send(a, t, 0, zn)

        @pl.when(c == a)
        def _():
            wcopy(a, t, 17, pair).start()

    def ring(a, k, other):
        slot = ring_slot(k, 1 - xl if other else xl, d)
        keeper = c == (1 if other else 0)
        arrived = wcopy(a, slot, 0, zn)
        onward = wcopy(a, slot, 4 * other + k if other else k, zn)
        across = wcopy(a, slot, 7 + 4 * other + k, sib)
        if k == 4:

            @pl.when(keeper)
            def _():
                arrived.wait_recv()
                across.start()

        elif k == 3:
            arrived.wait_recv()

            @pl.when(keeper)
            def _():
                onward.start()

            across.start()
            sent.append(across)
        elif k == 0:
            arrived.wait_recv()
            onward.start()
            sent.append(onward)
            across = wcopy(a, slot, 16, sib)

            @pl.when(c == a)
            def _():
                across.start()

        else:
            arrived.wait_recv()
            onward.start()
            across.start()
            sent.extend((onward, across))

    def ring_rest(a):
        for other in (0, 1):
            for k in range(1, 4):
                slot = ring_slot(k, 1 - xl if other else xl, -d)
                wcopy(a, slot, 0, zn).wait_recv()
        wcopy(a, ring_slot(4, lax.rem(xl + 1 - c, 2), d), 0, zn).wait_recv()

    def ring_end(a):
        @pl.when(c == a)
        def _():
            wcopy(a, t, 17, pair).wait_send()
            wcopy(a, t, 16, sib).wait_send()

        wcopy(a, t, 3 + 4 * c, zn).wait_send()
        wcopy(a, t, 11 + 4 * c, sib).wait_send()

    def gather_start(a):
        own[a].wait()

        @pl.when(c == 1)
        def _():
            wcopy(a, t, 3, zn).start()

        @pl.when(c == 0)
        def _():
            wcopy(a, t, 0, zn).start()
            wcopy(a, t, 4, xn).start()

    def gather_a(a, i):
        slot = mine(i, xl)
        if i == 0:

            @pl.when(c == 1)
            def _():
                wcopy(a, slot, 0, zn).wait_recv()
                wcopy(a, slot, 0, zn).start()
                wcopy(a, slot, 4, xn).start()
                wcopy(a, slot, 8, sib).start()

            return
        wcopy(a, slot, 0, zn).wait_recv()
        if i < 3:
            send(a, slot, i, zn)
        send(a, slot, 4 + i, xn)
        send(a, slot, 8 + i, sib)

    def gather_b(a, i):
        slot = mine(i, 1 - xl)
        wcopy(a, slot, 0, zn).wait_recv()
        send(a, slot, 12 + i, sib)

    def gather_rest(a):
        for i in range(4):
            slot = theirs(i, xl)
            if i == 0:

                @pl.when(c == 0)
                def _():
                    wcopy(a, slot, 0, zn).wait_recv()

            else:
                wcopy(a, slot, 0, zn).wait_recv()
            wcopy(a, theirs(i, 1 - xl), 0, zn).wait_recv()

    def gather_end(a):
        wcopy(a, mine(0, xl), 0, zn).wait_send()
        wcopy(a, mine(0, xl), 4, xn).wait_send()

        @pl.when(c == 1)
        def _():
            wcopy(a, t, 3, zn).wait_send()
            wcopy(a, mine(0, xl), 8, sib).wait_send()

    def arrange_in(source, target):
        @pl.loop(0, 8)
        def _(pair):
            rows = pl.ds(pl.multiple_of(pair * 144, 16), 144)
            both = jnp.concatenate(
                [source[2 * pair].astype(F32), source[2 * pair + 1].astype(F32)], axis=0
            )
            for part in range(3):
                cut = both[:, part * HD : (part + 1) * HD]
                wide = jnp.concatenate([cut, jnp.zeros((144, HP - HD), F32)], axis=1)
                target[part, rows, :] = wide.astype(BF)

    def arrange_out(source, target):
        for four in range(4):
            block = jnp.concatenate([source[4 * four + k].astype(F32) for k in range(4)], axis=0)
            target[144 * four : 144 * (four + 1), :] = block.astype(BF)
        target[HD:HP, :] = jnp.zeros((HP - HD, D), BF)

    ring_start(0)
    ring_start(1)

    steps = mod_ref.shape[1]
    chosen = (iota((6, steps, D), 1) == ts_ref[0]).astype(F32)
    modulators = jnp.sum(mod_ref[...] * chosen, axis=1)
    there = iota((TOK, TOK), 1)
    here = iota((TOK, TOK), 0)
    perm = (there == (here & 31) * COLS + (here >> 5)).astype(F32).astype(BF)
    ordered = dot(perm, lat_ref[...])
    latp[...] = ordered.astype(BF)
    xs[2] = (layer_norm(ordered) * (1.0 + modulators[1:2]) + modulators[0:1]).astype(BF)

    def scopy(source, hop, side):
        return pltpu.make_async_remote_copy(
            src_ref=xs.at[source], dst_ref=xs.at[2 - hop if side == 0 else 2 + hop],
            send_sem=s_send.at[2 * (hop - 1) + side], recv_sem=s_recv.at[2 * (hop - 1) + side],
            device_id=east if side == 0 else west, device_id_type=MESH,
        )

    def strip_send(hop):
        for side in (0, 1):
            source = 2 if hop == 1 else (1 if side == 0 else 3)
            if hop == 2:
                scopy(2, 1, side).wait_recv()
            copy = scopy(source, hop, side)
            copy.start()
            sent.append(copy)

    ring(0, 1, 0)
    ring(0, 0, 1)
    strip_send(1)

    kbuf[9 * COLS :] = jnp.zeros((COLS, ROWS, HP), BF)
    vbuf[9 * COLS :] = jnp.zeros((COLS, ROWS, HP), BF)

    lane = iota((HP, 128), 0)
    head = iota((HP, 128), 1) * HEAD_DIM
    seg[...] = ((lane >= head) & (lane < head + HEAD_DIM)).astype(F32).astype(BF)
    lane = iota((256, HP), 1)
    head = (iota((256, HP), 0) & 127) * HEAD_DIM
    seg_t[...] = ((lane >= head) & (lane < head + HEAD_DIM)).astype(F32).astype(BF)
    gpad[...] = jnp.zeros_like(gpad)
    gpad[0:2, 0:HEAD_DIM] = sg_ref[...]
    gpad[2:4, 0:HEAD_DIM] = tg_ref[...]
    lane = iota((128, HP), 1)
    within = lane
    for h in range(1, HEADS):
        within = jnp.where(lane >= h * HEAD_DIM, lane - h * HEAD_DIM, within)
    spread = (within == iota((128, HP), 0)).astype(F32)
    gains[...] = jnp.dot(
        gpad[...], spread, preferred_element_type=F32, precision=lax.Precision.HIGHEST
    )
    factor = HEAD_DIM ** (-0.5) * LOG2E

    ring(0, 2, 0)
    ring(1, 1, 0)
    ring(0, 1, 1)
    ring(1, 0, 1)
    ring(0, 3, 0)
    ring(1, 2, 0)
    strip_send(2)
    ring(0, 2, 1)
    ring(1, 1, 1)
    ring(0, 4, 0)
    ring(0, 3, 1)
    ring(1, 3, 0)
    ring(1, 2, 1)
    ring(0, 4, 1)
    ring_rest(0)
    arrange_in(w_si, w_spat)

    qbuf[...] = head_norm(dot(xs[2], w_spat[0]), gains[0:1] * factor, seg[...], seg_t[...])

    def keys_values(slot):
        cols = pl.ds(slot * (2 * COLS), COLS)
        x = xs[slot]
        keys = head_norm(dot(x, w_spat[1]), gains[1:2], seg[...], seg_t[...])
        kbuf[cols] = keys.reshape(COLS, ROWS, HP)
        vbuf[cols] = dot(x, w_spat[2]).astype(BF).reshape(COLS, ROWS, HP)

    def kv_copies(order):
        target = 2 * order + 1
        source = target + 1 - 2 * c
        src = pl.ds(source * COLS, COLS)
        dst = pl.ds(target * COLS, COLS)
        return [
            pltpu.make_async_remote_copy(
                src_ref=buf.at[src], dst_ref=buf.at[dst], send_sem=kv_send.at[j, order],
                recv_sem=kv_recv.at[j, order], device_id=sib, device_id_type=MESH,
            )
            for j, buf in enumerate((kbuf, vbuf))
        ]

    def kv_share(order):
        for copy in kv_copies(order):
            copy.start()
            sent.append(copy)

    keys_values(2)
    ring(1, 4, 0)
    ring(1, 3, 1)
    later = (2, 3)
    for a in later:
        gather_start(a)
    keys_values(1)
    ring(1, 4, 1)
    keys_values(3)

    kv_share(1)
    kv_share(2)
    kv_share(3 * c)

    def hop(i):
        for a in later:
            if i < 4:
                gather_a(a, i)
        for a in later:
            if i > 0:
                gather_b(a, i - 1)

    hop(0)
    for side in (0, 1):
        scopy(2, 2, side).wait_recv()
    keys_values(0)
    keys_values(4)

    kv_share(3 - 3 * c)
    hop(1)

    shift = lax.rem(COLS * l - off_ref[0] + STRIDE, STRIDE)
    table = iw_ref[...].astype(F32)
    place = iota((ROWS, WIN), 1)
    second, first = [], []
    for col in range(COLS):
        m = lax.rem(shift + col, STRIDE)
        second.append(jnp.sum(jnp.where(place == m, table, 0.0), axis=1, keepdims=True))
        first.append(jnp.sum(jnp.where(place == m + STRIDE, table, 0.0), axis=1, keepdims=True))
    second = jnp.concatenate(second, axis=0)
    first = jnp.concatenate(first, axis=0)
    share_first = first / (first + second)
    share_second = second / (first + second)
    early = (shift + (iota((TOK, 1), 0) >> 5)) < STRIDE

    for order in range(4):
        for copy in kv_copies(order):
            copy.wait_recv()

    CELL = STRIDE * ROWS
    for col in range(4 * STRIDE):
        rows = slice(col * ROWS, (col + 1) * ROWS)
        kcell[rows, :] = kbuf[col + STRIDE - shift]
        vcell[rows, :] = vbuf[col + STRIDE - shift]

    def window(h):
        w = (9 * h) // 16 * 128
        off = HEAD_DIM * h - w
        lanes = iota((1, 256), 1)
        inside = ((lanes >= off) & (lanes < off + HEAD_DIM)).astype(F32)
        return w, inside

    def spatial_head(h, _):
        w, inside = window(h)
        cols = pl.ds(w, 256)
        inside_b = inside.astype(BF)
        outside_b = (1.0 - inside).astype(BF)
        qh = qbuf[:, cols] * inside_b
        totals, sums = [], []
        for g in range(4):
            rows = slice(g * CELL, (g + 1) * CELL)
            powers = jnp.exp2(dot_t(qh, kcell[rows, cols])).astype(BF)
            o = dot(powers, vcell[rows, cols] * inside_b + outside_b)
            totals.append(o)
            sums.append(o[:, 255:256])
        near = sums[1] + sums[2]
        ca = share_first / jnp.where(early, sums[0] + sums[1], near)
        cb = share_second / jnp.where(early, near, sums[2] + sums[3])
        cab = ca + cb
        res = (
            jnp.where(early, ca, 0.0) * totals[0]
            + jnp.where(early, cab, ca) * totals[1]
            + jnp.where(early, cb, cab) * totals[2]
            + jnp.where(early, 0.0, cb) * totals[3]
        )
        att[:, cols] = att[:, cols] * (1.0 - inside) + res * inside
        return 0

    att[...] = jnp.zeros_like(att)
    for h in range(4):
        spatial_head(h, 0)
    hop(2)
    for h in range(4, 8):
        spatial_head(h, 0)
    hop(3)
    ring_rest(1)
    arrange_out(w_so, wo_spat)

    middle = latp[...].astype(F32) + modulators[2:3] * dot(att[...].astype(BF), wo_spat[...])
    middle = middle.astype(BF)
    mid[...] = middle
    normed = layer_norm(middle.astype(F32)) * (1.0 + modulators[4:5]) + modulators[3:4]
    nm[...] = normed.astype(BF)

    BAND = TOK // 16
    ORDER = (8, 9, 7, 10, 6, 11, 5, 12, 4, 13, 3, 14, 2, 15, 1)

    def band(index):
        return pl.ds(pl.multiple_of(index * BAND, BAND), BAND)

    def exchange(source, target, send_sems, recv_sems):
        for k in ORDER:
            peer = lax.rem(t + k, ntm)
            copy = pltpu.make_async_remote_copy(
                src_ref=source.at[band(peer)], dst_ref=target.at[band(t)],
                send_sem=send_sems.at[k], recv_sem=recv_sems.at[t],
                device_id=dev(peer, l), device_id_type=MESH,
            )
            copy.start()
            sent.append(copy)
        target[band(t), :] = source[band(t), :]

    def exchange_wait(source, target, send_sems, recv_sems):
        for k in range(1, 16):
            peer = lax.rem(t + k, ntm)
            pltpu.make_async_remote_copy(
                src_ref=source.at[band(peer)], dst_ref=target.at[band(peer)],
                send_sem=send_sems.at[k], recv_sem=recv_sems.at[peer],
                device_id=dev(peer, l), device_id_type=MESH,
            ).wait_recv()

    exchange(nm, xt, a_send, a_recv)
    for a in (2, 3):
        gather_b(a, 3)
    gather_rest(2)
    gather_rest(3)
    arrange_in(w_ti, w_temp)
    arrange_out(w_to, wo_temp)
    exchange_wait(nm, xt, a_send, a_recv)

    x = xt[...]
    tqkv[0] = head_norm(dot(x, w_temp[0]), gains[2:3] * factor, seg[...], seg_t[...])
    tqkv[1] = head_norm(dot(x, w_temp[1]), gains[3:4], seg[...], seg_t[...])
    tqkv[2] = dot(x, w_temp[2]).astype(BF)
    same = ((iota((TOK, TOK), 0) & 15) == (iota((TOK, TOK), 1) & 15)).astype(F32)

    def temporal_head(h, _):
        w, inside = window(h)
        cols = pl.ds(w, 256)
        inside_b = inside.astype(BF)
        outside_b = (1.0 - inside).astype(BF)
        scores = dot_t(tqkv[0, :, cols] * inside_b, tqkv[1, :, cols])
        powers = (jnp.exp2(scores) * same).astype(BF)
        o = dot(powers, tqkv[2, :, cols] * inside_b + outside_b)
        att[:, cols] = att[:, cols] * (1.0 - inside) + o * (inside / o[:, 255:256])
        return 0

    att[...] = jnp.zeros_like(att)
    for h in range(8):
        temporal_head(h, 0)
    tsend[...] = att[...].astype(BF)
    exchange(tsend, rt, r_send, r_recv)
    there = iota((TOK, TOK), 1)
    here = iota((TOK, TOK), 0)
    back = (there == (here & 7) * ROWS + (here >> 3)).astype(F32).astype(BF)
    exchange_wait(tsend, rt, r_send, r_recv)

    result = mid[...].astype(F32) + modulators[5:6] * dot(rt[...], wo_temp[...])
    out_ref[...] = dot(back, result.astype(BF)).astype(BF)

    for copy in sent:
        copy.wait_send()
    for a in (0, 1):
        ring_end(a)
    for a in later:
        gather_end(a)


def local(
    latent,
    timestep,
    modulation,
    window_offset,
    intersection_weight,
    spatial_in,
    spatial_gain,
    spatial_out,
    temporal_in,
    temporal_gain,
    temporal_out,
):
    vmem = pl.BlockSpec(memory_space=pltpu.VMEM)
    smem = pl.BlockSpec(memory_space=pltpu.SMEM)
    hbm = pl.BlockSpec(memory_space=pl.ANY)
    dma = pltpu.SemaphoreType.DMA
    out = pl.pallas_call(
        kernel,
        out_shape=jax.ShapeDtypeStruct((TOK, D), BF),
        in_specs=[vmem, smem, vmem, smem, vmem, hbm, vmem, hbm, hbm, vmem, hbm],
        out_specs=vmem,
        scratch_shapes=[
            pltpu.VMEM((16, 72, 3 * HD), BF),
            pltpu.VMEM((16, 36, D), BF),
            pltpu.VMEM((16, 72, 3 * HD), BF),
            pltpu.VMEM((16, 36, D), BF),
            pltpu.VMEM((3, D, HP), BF),
            pltpu.VMEM((3, D, HP), BF),
            pltpu.VMEM((HP, D), BF),
            pltpu.VMEM((HP, D), BF),
            pltpu.VMEM((HP, 128), BF),
            pltpu.VMEM((256, HP), BF),
            pltpu.VMEM((8, HP), F32),
            pltpu.VMEM((8, 128), F32),
            pltpu.VMEM((TOK, D), BF),
            pltpu.VMEM((5, TOK, D), BF),
            pltpu.VMEM((TOK, HP), BF),
            pltpu.VMEM((10 * COLS, ROWS, HP), BF),
            pltpu.VMEM((10 * COLS, ROWS, HP), BF),
            pltpu.VMEM((8 * TOK, HP), BF),
            pltpu.VMEM((8 * TOK, HP), BF),
            pltpu.VMEM((TOK, HP), F32),
            pltpu.VMEM((TOK, D), BF),
            pltpu.VMEM((TOK, D), BF),
            pltpu.VMEM((TOK, D), BF),
            pltpu.VMEM((3, TOK, HP), BF),
            pltpu.VMEM((TOK, HP), BF),
            pltpu.VMEM((TOK, HP), BF),
            dma((4, 18)),
            dma((4, 16)),
            dma((4,)),
            dma((4,)),
            dma((2, 4)),
            dma((2, 4)),
            dma((16,)),
            dma((16,)),
            dma((16,)),
            dma((16,)),
            dma((4,)),
        ],
        compiler_params=pltpu.CompilerParams(
            collective_id=0, has_side_effects=True, vmem_limit_bytes=56 << 20
        ),
        cost_estimate=pl.CostEstimate(
            flops=10 * 10**9, bytes_accessed=4 * 10**6, transcendentals=5 * 10**6
        ),
    )(
        latent.reshape(TOK, D),
        timestep,
        jnp.transpose(modulation, (1, 0, 2)),
        window_offset,
        intersection_weight,
        spatial_in,
        spatial_gain,
        spatial_out,
        temporal_in,
        temporal_gain,
        temporal_out,
    )
    return out.reshape(latent.shape)


def solution(mesh):
    in_specs = (
        P("tm", None, "lon", None),
        P(),
        P(),
        P("tm"),
        P(),
        P("tm", None),
        P(),
        P("tm", None),
        P("tm", None),
        P(),
        P("tm", None),
    )
    out_specs = P("tm", None, "lon", None)
    return jax.shard_map(local, mesh=mesh, in_specs=in_specs, out_specs=out_specs, check_vma=False)
```

```python
import functools
import math

import jax
import jax.numpy as jnp
from jax import lax
from jax.experimental import pallas as pl
from jax.experimental.pallas import tpu as pltpu
from jax.sharding import PartitionSpec as P

D = 1152
HEADS = 8
HEAD_DIM = 72
HD = 576
HP = 640
ROWS = 32
COLS = 8
TOK = ROWS * COLS
WIN = 32
STRIDE = 16
BF = jnp.bfloat16
F32 = jnp.float32
MESH = pl.DeviceIdType.MESH
LOG2E = math.log2(math.e)


def iota(shape, dim):
    return lax.broadcasted_iota(jnp.int32, shape, dim)


def dot(a, b):
    return jnp.dot(a, b, preferred_element_type=F32)


def dot_t(a, b):
    return lax.dot_general(a, b, (((1,), (1,)), ((), ())), preferred_element_type=F32)


def layer_norm(x):
    center = x - jnp.mean(x, axis=-1, keepdims=True)
    spread = jnp.mean(center * center, axis=-1, keepdims=True)
    return center * lax.rsqrt(spread + 1e-06)


def head_norm(p, gain, seg, seg_t):
    square = dot((p * p).astype(BF), seg) * (1.0 / HEAD_DIM) + 1e-06
    inverse = lax.rsqrt(square)
    high = inverse.astype(BF)
    low = (inverse - high.astype(F32)).astype(BF)
    spread = dot(jnp.concatenate([high, low], axis=1), seg_t)
    return (p * spread * gain).astype(BF)


def kernel(
    lat_ref, ts_ref, mod_ref, off_ref, iw_ref, si_ref, sg_ref, so_ref, ti_ref, tg_ref, to_ref,
    out_ref,
    w_si, w_so, w_ti, w_to, w_spat, w_temp, wo_spat, wo_temp,
    seg, seg_t, gains, gpad, latp, xs, qbuf, kbuf, vbuf, kcell, vcell, att, mid, nm, xt, tqkv, tsend, rt,
    w_send, w_recv, s_send, s_recv, kv_send, kv_recv, a_send, a_recv, r_send, r_recv, loc,
):
    t = lax.axis_index("tm")
    l = lax.axis_index("lon")
    nlon = lax.axis_size("lon")
    ntm = lax.axis_size("tm")
    nz, nq = ntm // 2, nlon // 2
    ny = nq // 2
    z, xl = t // 2, lax.rem(t, 2)
    q, c = l // 2, lax.rem(l, 2)
    xh, y = q // ny, lax.rem(q, ny)
    d = 1 - 2 * c

    def dev(tm, lon):
        return {"tm": tm, "lon": lon}

    def around(step):
        x = lax.rem(xh * 2 + xl + step + 4, 4)
        return dev(z * 2 + lax.rem(x, 2), ((x // 2) * ny + y) * 2 + c)

    zn = dev(lax.rem(z + d + nz, nz) * 2 + xl, l)
    xn = around(d)
    xp = around(-d)
    sib = dev(t, q * 2 + 1 - c)
    east = dev(t, lax.rem(q + 1, nq) * 2 + c)
    west = dev(t, lax.rem(q + nq - 1, nq) * 2 + c)

    barrier = pltpu.get_barrier_semaphore()
    others = [dev(lax.rem(t + k, ntm), l) for k in range(1, 16)] + [sib, east, west]
    across_x = lax.rem(xh * 2 + xl + jnp.where(xl == 0, 3, 1), 4)
    across = dev(z * 2 + lax.rem(across_x, 2), ((across_x // 2) * ny + y) * 2 + c)
    others.append(across)
    for other in others:
        pl.semaphore_signal(barrier, inc=1, device_id=other, device_id_type=MESH)

    weights = (w_si, w_so, w_ti, w_to)
    sources = (si_ref, so_ref, ti_ref, to_ref)
    own = [pltpu.make_async_copy(sources[a], weights[a].at[t], loc.at[a]) for a in range(4)]
    for copy in own:
        copy.start()

    pl.semaphore_wait(barrier, len(others))

    sent = []

    def wcopy(a, slot, sem, target):
        return pltpu.make_async_remote_copy(
            src_ref=weights[a].at[slot], dst_ref=weights[a].at[slot],
            send_sem=w_send.at[a, sem], recv_sem=w_recv.at[a, slot],
            device_id=target, device_id_type=MESH,
        )

    def mine(i, plane):
        return lax.rem(z - d * (i + c) + 2 * nz, nz) * 2 + plane

    def theirs(i, plane):
        return lax.rem(z + d * (i + 1 - c) + 2 * nz, nz) * 2 + plane

    def send(a, slot, sem, target):
        copy = wcopy(a, slot, sem, target)
        copy.start()
        sent.append(copy)

    pair = dev(z * 2 + 1 - xl, l)

    def ring_slot(k, plane, way):
        return lax.rem(z - way * k + 2 * nz, nz) * 2 + plane

    def ring_start(a):
        own[a].wait()
        send(a, t, 0, zn)

        @pl.when(c == a)
        def _():
            wcopy(a, t, 17, pair).start()

    def ring(a, k, other):
        slot = ring_slot(k, 1 - xl if other else xl, d)
        keeper = c == (1 if other else 0)
        arrived = wcopy(a, slot, 0, zn)
        onward = wcopy(a, slot, 4 * other + k if other else k, zn)
        across = wcopy(a, slot, 7 + 4 * other + k, sib)
        if k == 4:

            @pl.when(keeper)
            def _():
                arrived.wait_recv()
                across.start()

        elif k == 3:
            arrived.wait_recv()

            @pl.when(keeper)
            def _():
                onward.start()

            across.start()
            sent.append(across)
        elif k == 0:
            arrived.wait_recv()
            onward.start()
            sent.append(onward)
            across = wcopy(a, slot, 16, sib)

            @pl.when(c == a)
            def _():
                across.start()

        else:
            arrived.wait_recv()
            onward.start()
            across.start()
            sent.extend((onward, across))

    def ring_rest(a):
        for other in (0, 1):
            for k in range(1, 4):
                slot = ring_slot(k, 1 - xl if other else xl, -d)
                wcopy(a, slot, 0, zn).wait_recv()
        wcopy(a, ring_slot(4, lax.rem(xl + 1 - c, 2), d), 0, zn).wait_recv()

    def ring_end(a):
        @pl.when(c == a)
        def _():
            wcopy(a, t, 17, pair).wait_send()
            wcopy(a, t, 16, sib).wait_send()

        wcopy(a, t, 3 + 4 * c, zn).wait_send()
        wcopy(a, t, 11 + 4 * c, sib).wait_send()

    def gather_start(a):
        own[a].wait()

        @pl.when(c == 1)
        def _():
            wcopy(a, t, 3, zn).start()

        @pl.when(c == 0)
        def _():
            wcopy(a, t, 0, zn).start()
            wcopy(a, t, 4, xn).start()

    def gather_a(a, i):
        slot = mine(i, xl)
        if i == 0:

            @pl.when(c == 1)
            def _():
                wcopy(a, slot, 0, zn).wait_recv()
                wcopy(a, slot, 0, zn).start()
                wcopy(a, slot, 4, xn).start()
                wcopy(a, slot, 8, sib).start()

            return
        wcopy(a, slot, 0, zn).wait_recv()
        if i < 3:
            send(a, slot, i, zn)
        send(a, slot, 4 + i, xn)
        send(a, slot, 8 + i, sib)

    def gather_b(a, i):
        slot = mine(i, 1 - xl)
        wcopy(a, slot, 0, zn).wait_recv()
        send(a, slot, 12 + i, sib)

    def gather_rest(a):
        for i in range(4):
            slot = theirs(i, xl)
            if i == 0:

                @pl.when(c == 0)
                def _():
                    wcopy(a, slot, 0, zn).wait_recv()

            else:
                wcopy(a, slot, 0, zn).wait_recv()
            wcopy(a, theirs(i, 1 - xl), 0, zn).wait_recv()

    def gather_end(a):
        wcopy(a, mine(0, xl), 0, zn).wait_send()
        wcopy(a, mine(0, xl), 4, xn).wait_send()

        @pl.when(c == 1)
        def _():
            wcopy(a, t, 3, zn).wait_send()
            wcopy(a, mine(0, xl), 8, sib).wait_send()

    def arrange_in(source, target):
        @pl.loop(0, 8)
        def _(pair):
            rows = pl.ds(pl.multiple_of(pair * 144, 16), 144)
            both = jnp.concatenate(
                [source[2 * pair].astype(F32), source[2 * pair + 1].astype(F32)], axis=0
            )
            for part in range(3):
                cut = both[:, part * HD : (part + 1) * HD]
                wide = jnp.concatenate([cut, jnp.zeros((144, HP - HD), F32)], axis=1)
                target[part, rows, :] = wide.astype(BF)

    def arrange_out(source, target):
        for four in range(4):
            block = jnp.concatenate([source[4 * four + k].astype(F32) for k in range(4)], axis=0)
            target[144 * four : 144 * (four + 1), :] = block.astype(BF)
        target[HD:HP, :] = jnp.zeros((HP - HD, D), BF)

    ring_start(0)
    ring_start(1)

    steps = mod_ref.shape[1]
    chosen = (iota((6, steps, D), 1) == ts_ref[0]).astype(F32)
    modulators = jnp.sum(mod_ref[...] * chosen, axis=1)
    there = iota((TOK, TOK), 1)
    here = iota((TOK, TOK), 0)
    perm = (there == (here & 31) * COLS + (here >> 5)).astype(F32).astype(BF)
    ordered = dot(perm, lat_ref[...])
    latp[...] = ordered.astype(BF)
    xs[2] = (layer_norm(ordered) * (1.0 + modulators[1:2]) + modulators[0:1]).astype(BF)

    def scopy(source, hop, side):
        return pltpu.make_async_remote_copy(
            src_ref=xs.at[source], dst_ref=xs.at[2 - hop if side == 0 else 2 + hop],
            send_sem=s_send.at[2 * (hop - 1) + side], recv_sem=s_recv.at[2 * (hop - 1) + side],
            device_id=east if side == 0 else west, device_id_type=MESH,
        )

    def strip_send(hop):
        for side in (0, 1):
            source = 2 if hop == 1 else (1 if side == 0 else 3)
            if hop == 2:
                scopy(2, 1, side).wait_recv()
            copy = scopy(source, hop, side)
            copy.start()
            sent.append(copy)

    ring(0, 1, 0)
    ring(0, 0, 1)
    strip_send(1)

    kbuf[9 * COLS :] = jnp.zeros((COLS, ROWS, HP), BF)
    vbuf[9 * COLS :] = jnp.zeros((COLS, ROWS, HP), BF)

    lane = iota((HP, 128), 0)
    head = iota((HP, 128), 1) * HEAD_DIM
    seg[...] = ((lane >= head) & (lane < head + HEAD_DIM)).astype(F32).astype(BF)
    lane = iota((256, HP), 1)
    head = (iota((256, HP), 0) & 127) * HEAD_DIM
    seg_t[...] = ((lane >= head) & (lane < head + HEAD_DIM)).astype(F32).astype(BF)
    gpad[...] = jnp.zeros_like(gpad)
    gpad[0:2, 0:HEAD_DIM] = sg_ref[...]
    gpad[2:4, 0:HEAD_DIM] = tg_ref[...]
    lane = iota((128, HP), 1)
    within = lane
    for h in range(1, HEADS):
        within = jnp.where(lane >= h * HEAD_DIM, lane - h * HEAD_DIM, within)
    spread = (within == iota((128, HP), 0)).astype(F32)
    gains[...] = jnp.dot(
        gpad[...], spread, preferred_element_type=F32, precision=lax.Precision.HIGHEST
    )
    factor = HEAD_DIM ** (-0.5) * LOG2E

    ring(0, 2, 0)
    ring(1, 1, 0)
    ring(0, 1, 1)
    ring(1, 0, 1)
    ring(0, 3, 0)
    ring(1, 2, 0)
    strip_send(2)
    ring(0, 2, 1)
    ring(1, 1, 1)
    ring(0, 4, 0)
    ring(0, 3, 1)
    ring(1, 3, 0)
    ring(1, 2, 1)
    ring(0, 4, 1)
    ring_rest(0)
    arrange_in(w_si, w_spat)

    qbuf[...] = head_norm(dot(xs[2], w_spat[0]), gains[0:1] * factor, seg[...], seg_t[...])

    def keys_values(slot):
        cols = pl.ds(slot * (2 * COLS), COLS)
        x = xs[slot]
        keys = head_norm(dot(x, w_spat[1]), gains[1:2], seg[...], seg_t[...])
        kbuf[cols] = keys.reshape(COLS, ROWS, HP)
        vbuf[cols] = dot(x, w_spat[2]).astype(BF).reshape(COLS, ROWS, HP)

    def kv_copies(order):
        target = 2 * order + 1
        source = target + 1 - 2 * c
        src = pl.ds(source * COLS, COLS)
        dst = pl.ds(target * COLS, COLS)
        return [
            pltpu.make_async_remote_copy(
                src_ref=buf.at[src], dst_ref=buf.at[dst], send_sem=kv_send.at[j, order],
                recv_sem=kv_recv.at[j, order], device_id=sib, device_id_type=MESH,
            )
            for j, buf in enumerate((kbuf, vbuf))
        ]

    def kv_share(order):
        for copy in kv_copies(order):
            copy.start()
            sent.append(copy)

    keys_values(2)
    ring(1, 4, 0)
    ring(1, 3, 1)
    later = (2, 3)
    for a in later:
        gather_start(a)
    keys_values(1)
    ring(1, 4, 1)
    keys_values(3)

    kv_share(1)
    kv_share(2)
    kv_share(3 * c)

    def hop(i):
        for a in later:
            if i < 4:
                gather_a(a, i)
        for a in later:
            if i > 0:
                gather_b(a, i - 1)

    hop(0)
    for side in (0, 1):
        scopy(2, 2, side).wait_recv()
    keys_values(0)
    keys_values(4)

    kv_share(3 - 3 * c)
    hop(1)

    shift = lax.rem(COLS * l - off_ref[0] + STRIDE, STRIDE)
    table = iw_ref[...].astype(F32)
    place = iota((ROWS, WIN), 1)
    second, first = [], []
    for col in range(COLS):
        m = lax.rem(shift + col, STRIDE)
        second.append(jnp.sum(jnp.where(place == m, table, 0.0), axis=1, keepdims=True))
        first.append(jnp.sum(jnp.where(place == m + STRIDE, table, 0.0), axis=1, keepdims=True))
    second = jnp.concatenate(second, axis=0)
    first = jnp.concatenate(first, axis=0)
    share_first = first / (first + second)
    share_second = second / (first + second)
    early = (shift + (iota((TOK, 1), 0) >> 5)) < STRIDE

    for order in range(4):
        for copy in kv_copies(order):
            copy.wait_recv()

    CELL = STRIDE * ROWS
    for col in range(4 * STRIDE):
        rows = slice(col * ROWS, (col + 1) * ROWS)
        kcell[rows, :] = kbuf[col + STRIDE - shift]
        vcell[rows, :] = vbuf[col + STRIDE - shift]

    def window(h):
        w = (9 * h) // 16 * 128
        off = HEAD_DIM * h - w
        lanes = iota((1, 256), 1)
        inside = ((lanes >= off) & (lanes < off + HEAD_DIM)).astype(F32)
        return w, inside

    def spatial_head(h, _):
        w, inside = window(h)
        cols = pl.ds(w, 256)
        inside_b = inside.astype(BF)
        outside_b = (1.0 - inside).astype(BF)
        qh = qbuf[:, cols] * inside_b
        totals, sums = [], []
        for g in range(4):
            rows = slice(g * CELL, (g + 1) * CELL)
            powers = jnp.exp2(dot_t(qh, kcell[rows, cols])).astype(BF)
            o = dot(powers, vcell[rows, cols] * inside_b + outside_b)
            totals.append(o)
            sums.append(o[:, 255:256])
        near = sums[1] + sums[2]
        ca = share_first / jnp.where(early, sums[0] + sums[1], near)
        cb = share_second / jnp.where(early, near, sums[2] + sums[3])
        cab = ca + cb
        res = (
            jnp.where(early, ca, 0.0) * totals[0]
            + jnp.where(early, cab, ca) * totals[1]
            + jnp.where(early, cb, cab) * totals[2]
            + jnp.where(early, 0.0, cb) * totals[3]
        )
        att[:, cols] = att[:, cols] * (1.0 - inside) + res * inside
        return 0

    att[...] = jnp.zeros_like(att)
    for h in range(4):
        spatial_head(h, 0)
    hop(2)
    for h in range(4, 8):
        spatial_head(h, 0)
    ring_rest(1)
    arrange_out(w_so, wo_spat)

    middle = latp[...].astype(F32) + modulators[2:3] * dot(att[...].astype(BF), wo_spat[...])
    middle = middle.astype(BF)
    mid[...] = middle
    normed = layer_norm(middle.astype(F32)) * (1.0 + modulators[4:5]) + modulators[3:4]
    nm[...] = normed.astype(BF)

    BAND = TOK // 16
    ORDER = (8, 9, 7, 10, 6, 11, 5, 12, 4, 13, 3, 14, 2, 15, 1)

    def band(index):
        return pl.ds(pl.multiple_of(index * BAND, BAND), BAND)

    def exchange(source, target, send_sems, recv_sems):
        for k in ORDER:
            peer = lax.rem(t + k, ntm)
            copy = pltpu.make_async_remote_copy(
                src_ref=source.at[band(peer)], dst_ref=target.at[band(t)],
                send_sem=send_sems.at[k], recv_sem=recv_sems.at[t],
                device_id=dev(peer, l), device_id_type=MESH,
            )
            copy.start()
            sent.append(copy)
        target[band(t), :] = source[band(t), :]

    def exchange_wait(source, target, send_sems, recv_sems):
        for k in range(1, 16):
            peer = lax.rem(t + k, ntm)
            pltpu.make_async_remote_copy(
                src_ref=source.at[band(peer)], dst_ref=target.at[band(peer)],
                send_sem=send_sems.at[k], recv_sem=recv_sems.at[peer],
                device_id=dev(peer, l), device_id_type=MESH,
            ).wait_recv()

    exchange(nm, xt, a_send, a_recv)
    hop(3)
    for a in (2, 3):
        gather_b(a, 3)
    gather_rest(2)
    gather_rest(3)
    arrange_in(w_ti, w_temp)
    arrange_out(w_to, wo_temp)
    exchange_wait(nm, xt, a_send, a_recv)

    x = xt[...]
    tqkv[0] = head_norm(dot(x, w_temp[0]), gains[2:3] * factor, seg[...], seg_t[...])
    tqkv[1] = head_norm(dot(x, w_temp[1]), gains[3:4], seg[...], seg_t[...])
    tqkv[2] = dot(x, w_temp[2]).astype(BF)
    same = ((iota((TOK, TOK), 0) & 15) == (iota((TOK, TOK), 1) & 15)).astype(F32)

    def temporal_head(h, _):
        w, inside = window(h)
        cols = pl.ds(w, 256)
        inside_b = inside.astype(BF)
        outside_b = (1.0 - inside).astype(BF)
        scores = dot_t(tqkv[0, :, cols] * inside_b, tqkv[1, :, cols])
        powers = (jnp.exp2(scores) * same).astype(BF)
        o = dot(powers, tqkv[2, :, cols] * inside_b + outside_b)
        att[:, cols] = att[:, cols] * (1.0 - inside) + o * (inside / o[:, 255:256])
        return 0

    att[...] = jnp.zeros_like(att)
    for h in range(8):
        temporal_head(h, 0)
    tsend[...] = att[...].astype(BF)
    exchange(tsend, rt, r_send, r_recv)
    there = iota((TOK, TOK), 1)
    here = iota((TOK, TOK), 0)
    back = (there == (here & 7) * ROWS + (here >> 3)).astype(F32).astype(BF)
    exchange_wait(tsend, rt, r_send, r_recv)

    result = mid[...].astype(F32) + modulators[5:6] * dot(rt[...], wo_temp[...])
    out_ref[...] = dot(back, result.astype(BF)).astype(BF)

    for copy in sent:
        copy.wait_send()
    for a in (0, 1):
        ring_end(a)
    for a in later:
        gather_end(a)


def local(
    latent,
    timestep,
    modulation,
    window_offset,
    intersection_weight,
    spatial_in,
    spatial_gain,
    spatial_out,
    temporal_in,
    temporal_gain,
    temporal_out,
):
    vmem = pl.BlockSpec(memory_space=pltpu.VMEM)
    smem = pl.BlockSpec(memory_space=pltpu.SMEM)
    hbm = pl.BlockSpec(memory_space=pl.ANY)
    dma = pltpu.SemaphoreType.DMA
    out = pl.pallas_call(
        kernel,
        out_shape=jax.ShapeDtypeStruct((TOK, D), BF),
        in_specs=[vmem, smem, vmem, smem, vmem, hbm, vmem, hbm, hbm, vmem, hbm],
        out_specs=vmem,
        scratch_shapes=[
            pltpu.VMEM((16, 72, 3 * HD), BF),
            pltpu.VMEM((16, 36, D), BF),
            pltpu.VMEM((16, 72, 3 * HD), BF),
            pltpu.VMEM((16, 36, D), BF),
            pltpu.VMEM((3, D, HP), BF),
            pltpu.VMEM((3, D, HP), BF),
            pltpu.VMEM((HP, D), BF),
            pltpu.VMEM((HP, D), BF),
            pltpu.VMEM((HP, 128), BF),
            pltpu.VMEM((256, HP), BF),
            pltpu.VMEM((8, HP), F32),
            pltpu.VMEM((8, 128), F32),
            pltpu.VMEM((TOK, D), BF),
            pltpu.VMEM((5, TOK, D), BF),
            pltpu.VMEM((TOK, HP), BF),
            pltpu.VMEM((10 * COLS, ROWS, HP), BF),
            pltpu.VMEM((10 * COLS, ROWS, HP), BF),
            pltpu.VMEM((8 * TOK, HP), BF),
            pltpu.VMEM((8 * TOK, HP), BF),
            pltpu.VMEM((TOK, HP), F32),
            pltpu.VMEM((TOK, D), BF),
            pltpu.VMEM((TOK, D), BF),
            pltpu.VMEM((TOK, D), BF),
            pltpu.VMEM((3, TOK, HP), BF),
            pltpu.VMEM((TOK, HP), BF),
            pltpu.VMEM((TOK, HP), BF),
            dma((4, 18)),
            dma((4, 16)),
            dma((4,)),
            dma((4,)),
            dma((2, 4)),
            dma((2, 4)),
            dma((16,)),
            dma((16,)),
            dma((16,)),
            dma((16,)),
            dma((4,)),
        ],
        compiler_params=pltpu.CompilerParams(
            collective_id=0, has_side_effects=True, vmem_limit_bytes=56 << 20
        ),
        cost_estimate=pl.CostEstimate(
            flops=10 * 10**9, bytes_accessed=4 * 10**6, transcendentals=5 * 10**6
        ),
    )(
        latent.reshape(TOK, D),
        timestep,
        jnp.transpose(modulation, (1, 0, 2)),
        window_offset,
        intersection_weight,
        spatial_in,
        spatial_gain,
        spatial_out,
        temporal_in,
        temporal_gain,
        temporal_out,
    )
    return out.reshape(latent.shape)


def solution(mesh):
    in_specs = (
        P("tm", None, "lon", None),
        P(),
        P(),
        P("tm"),
        P(),
        P("tm", None),
        P(),
        P("tm", None),
        P("tm", None),
        P(),
        P("tm", None),
    )
    out_specs = P("tm", None, "lon", None)
    return jax.shard_map(local, mesh=mesh, in_specs=in_specs, out_specs=out_specs, check_vma=False)
```
